256 devices in a mesh: blk: 128 (over y, z, x_lo, core), tp: 2 (over x_hi).
Axes of the slice: x: 4 (x_hi: 2, x_lo: 2; x = x_hi * 2 + x_lo), y: 4, z: 8, core: 2. Of those that a mesh axis runs over, the one named last changes fastest.
Arguments:
- queries: bfloat16 [65536, 2560], P('blk', 'tp'), may hold values from -128 to 128
- keys: bfloat16 [65536, 2560], P('blk', 'tp'), may hold values from -5.1 to 5.1
- values: bfloat16 [65536, 2560], P('blk', 'tp'), may hold values from -6 to 6
- positions: int32 [65536], P('blk'), may hold values from 0 to 511, as said below
- out_weight: bfloat16 [2560, 2560], P('blk', 'tp'), may hold values from -0.125 to 0.125
- cotangent: bfloat16 [65536, 2560], P('blk', 'tp'), may hold values from -24 to 24
Outputs:
- projected: bfloat16 [65536, 2560], P('blk', 'tp')
- weight_grad: float32 [2560, 2560], P('blk', 'tp')
- grad_queries: bfloat16 [65536, 2560], P('blk', 'tp')
- grad_keys: bfloat16 [65536, 2560], P('blk', 'tp')
- grad_values: bfloat16 [65536, 2560], P('blk', 'tp')
The draws below stay inside these ranges and needn't reach their ends.
Inputs may be any that keep to these rules, and one draw needn't show every extreme that they name: `positions`: each micro-batch of 512 tokens packs whole documents: a position is 0 at a document's first token and rises by one along it; documents begin only at local rows that are multiples of 16, and at least one micro-batch is a single document.
All inputs are finite; a program needn't handle non-finite values.
Results may differ from the reference program's by a relative error of at most 0.029.
Values may be sent and summed in bfloat16 or wider, within the bound.
No kernel may reach another device: no remote copies, remote signals or barrier semaphores. Data moves between devices by JAX's collectives and lax.ppermute only.
A program may use at most 128 MiB of HBM per device.

```python
import math
import jax
import jax.numpy as jnp
from jax import lax

D = 2560
HEADS = 20
HD = 128
TOK_DEV = 512
TOKENS = 65536


def shared_keys(key):
    return jnp.clip(jax.random.normal(key, (TOKENS, HEADS * HD), jnp.float32), -5.0, 5.0)


def draw_keys(key, part):
    base_draw = shared_keys(key)
    return base_draw.astype(jnp.bfloat16)


def draw_queries(key, part):
    key = jax.random.fold_in(key, 5)
    fresh = jnp.clip(jax.random.normal(key, (TOKENS, HEADS * HD), jnp.float32), -5.0, 5.0)
    return fresh.astype(jnp.bfloat16)


def draw_positions(key, part):
    key = jax.random.fold_in(key, 7)
    row_number = jnp.arange(TOKENS, dtype=jnp.int32)
    local_row = row_number % TOK_DEV
    micro_batch = row_number // TOK_DEV
    chosen = jax.random.randint(jax.random.fold_in(key, 1), (), 0, TOKENS // TOK_DEV)
    restart_draw = jax.random.randint(key, (TOKENS,), 0, 8)
    start_rows = (local_row == 0) | (local_row % 16 == 0) & (restart_draw == 0) & (micro_batch != chosen)
    marked = jnp.where(start_rows, row_number, 0)
    last_start = lax.cummax(marked, axis=0)
    return (row_number - last_start).astype(jnp.int32)


def spiked(values, stream_key, source, target, parts, factor):
    def block_of(position):
        return (jnp.arange(values.shape[position]) // (values.shape[position] // parts)).reshape((-1,) + (1,) * (values.ndim - 1 - position))

    first = jax.random.permutation(stream_key, parts)[block_of(target)]
    second = (block_of(target) + parts // 2) % parts
    return jnp.where((block_of(source) == first) | (block_of(source) == second), factor * values, values)


def block_scale(own_key, extent, cuts, least, top_value):
    def one(axis_at, blocks):
        steps = jax.random.uniform(jax.random.fold_in(jax.random.fold_in(own_key, 6), axis_at), (blocks,), jnp.float32, least / len(cuts), top_value / len(cuts))
        return jnp.repeat(jnp.exp(steps), extent[axis_at] // blocks).reshape((-1,) + (1,) * (len(extent) - axis_at - 1))

    level = one(*cuts[0])
    for cut in cuts[1:]:
        level = level * one(*cut)
    return level


def noise(rng, shape, deviation, most, pieces=(), kind=jnp.bfloat16):
    loudness = block_scale(rng, shape, pieces, -0.22, 0.18) if pieces else 1.0
    result = jax.random.normal(rng, shape, jnp.float32) * deviation * loudness
    return jnp.minimum(jnp.maximum(result, -most), most).astype(kind)


def gaussian_with(stream_key, shape, spread, most, split, heavy, kind=jnp.bfloat16):
    values = spread * jax.random.normal(stream_key, shape, jnp.float32)
    if split:
        values = values * block_scale(stream_key, shape, split, -0.22, 0.18)
    return jnp.clip(spiked(values, jax.random.fold_in(stream_key, 3), *heavy), -most, most).astype(kind)


def setup_inputs(seed: int = 0) -> dict:
    key_list = jax.random.split(jax.random.key(seed), 7)
    queries = draw_queries(jax.random.fold_in(key_list[6], 71), 0)
    keys = draw_keys(jax.random.fold_in(key_list[6], 71), 0)
    values = noise(key_list[2], (TOKENS, HEADS * HD), 1.0, 6.0, ((0, 128), (1, 2)))
    positions = draw_positions(jax.random.fold_in(key_list[6], 71), 0)
    out_weight = noise(key_list[4], (D, HEADS * HD), (HEADS * HD) ** -0.5, 0.125, ((0, 128), (1, 2)))
    cotangent = gaussian_with(key_list[5], (TOKENS, D), 1.0, 24.0, ((0, 128), (1, 2)), (0, 1, 128, 5.5))
    return dict(queries=queries, keys=keys, values=values, positions=positions, out_weight=out_weight, cotangent=cotangent)


def split_heads(matrix):
    length = matrix.shape[0]
    return matrix.reshape(length, matrix.shape[1] // HD, HD).astype(jnp.float32)

def attend(queries, keys, values, positions):
    length = queries.shape[0]
    score_scale = 1.0 / math.sqrt(HD)
    query_heads = split_heads(queries)
    key_heads = split_heads(keys)
    value_heads = split_heads(values)
    scores = jnp.einsum('qhd,khd->hqk', query_heads, key_heads) * score_scale
    row_index = jnp.arange(length, dtype=jnp.int32)[:, None]
    col_index = jnp.arange(length, dtype=jnp.int32)[None, :]
    visible = (col_index <= row_index) & (col_index >= row_index - positions[:, None])
    scores = jnp.where(visible[None], scores, -jnp.inf)
    row_top = lax.optimization_barrier(jnp.max(scores, axis=-1, keepdims=True))
    exponentials = jnp.exp(scores - row_top)
    probabilities = (exponentials / lax.optimization_barrier(jnp.sum(exponentials, axis=-1, keepdims=True))).astype(jnp.bfloat16)
    probabilities = lax.optimization_barrier(probabilities)
    attended = jnp.einsum('hqk,khd->qhd', probabilities.astype(jnp.float32), value_heads)
    attended = lax.optimization_barrier(attended.astype(jnp.bfloat16).reshape(length, -1))
    return (probabilities, attended)

def attend_back(queries, keys, values, probabilities, attended, grad_attended):
    length = queries.shape[0]
    score_scale = 1.0 / math.sqrt(HD)
    query_heads = split_heads(queries)
    key_heads = split_heads(keys)
    value_heads = split_heads(values)
    grad_heads = split_heads(grad_attended)
    attended_heads = split_heads(attended)
    prob_float = probabilities.astype(jnp.float32)
    grad_values = jnp.einsum('hqk,qhd->khd', prob_float, grad_heads).astype(jnp.bfloat16).reshape(length, -1)
    row_delta = jnp.transpose(lax.optimization_barrier(jnp.sum(grad_heads * attended_heads, axis=-1)))[:, :, None]
    grad_probs = jnp.einsum('qhd,khd->hqk', grad_heads, value_heads)
    grad_scores = (score_scale * prob_float * (grad_probs - row_delta)).astype(jnp.bfloat16)
    grad_scores = lax.optimization_barrier(grad_scores).astype(jnp.float32)
    grad_queries = jnp.einsum('hqk,khd->qhd', grad_scores, key_heads).astype(jnp.bfloat16).reshape(length, -1)
    grad_keys = jnp.einsum('hqk,qhd->khd', grad_scores, query_heads).astype(jnp.bfloat16).reshape(length, -1)
    return (grad_queries, grad_keys, grad_values)

def reference(queries, keys, values, positions, out_weight, cotangent):
    blocks = TOKENS // TOK_DEV

    def one_block(grad_total, block_index):
        first_row = (block_index * TOK_DEV).astype(jnp.int32)

        def take(array):
            return lax.dynamic_slice_in_dim(array, first_row, TOK_DEV, 0)
        query_rows = take(queries)
        key_rows = take(keys)
        value_rows = take(values)
        cot_rows = take(cotangent)
        probabilities, attended = attend(query_rows, key_rows, value_rows, take(positions))
        projected = jnp.dot(attended, out_weight.T, preferred_element_type=jnp.float32).astype(jnp.bfloat16)
        grad_attended = jnp.dot(cot_rows, out_weight, preferred_element_type=jnp.float32).astype(jnp.bfloat16)
        grad_total = grad_total + jnp.dot(cot_rows.T, attended, preferred_element_type=jnp.float32)
        grad_queries, grad_keys, grad_values = attend_back(query_rows, key_rows, value_rows, probabilities, attended, grad_attended)
        return (grad_total, (projected, grad_queries, grad_keys, grad_values))
    start_total = jnp.zeros((D, HEADS * HD), jnp.float32)
    weight_grad, stacked = lax.scan(one_block, start_total, jnp.arange(blocks, dtype=jnp.int32))
    projected, grad_queries, grad_keys, grad_values = [item.reshape(TOKENS, -1) for item in stacked]
    return (projected, weight_grad, grad_queries, grad_keys, grad_values)
```

```python
import functools
import math

import jax
import jax.numpy as jnp
from jax import lax
from jax.experimental import pallas as pl
from jax.experimental.pallas import tpu as pltpu
from jax.sharding import PartitionSpec as P

HD = 128
NY, NZ, NX, NC = 4, 8, 2, 2
BF = jnp.bfloat16
F32 = jnp.float32
NT = (((1,), (1,)), ((), ()))
TN = (((0,), (0,)), ((), ()))
CUT = 384
QB = 256


def dot(a, b, dims=(((1,), (0,)), ((), ()))):
    return lax.dot_general(a, b, dims, preferred_element_type=F32)


def attend_kernel(pos_ref, q_ref, k_ref, v_ref, att_ref, p_ref):
    length = q_ref.shape[0]
    for i in range(length // QB):
        rows = slice(i * QB, (i + 1) * QB)
        n = (i + 1) * QB
        s = dot(q_ref[rows, :], k_ref[:n, :], NT) * (1.0 / math.sqrt(HD))
        row = lax.broadcasted_iota(jnp.int32, (QB, n), 0) + i * QB
        col = lax.broadcasted_iota(jnp.int32, (QB, n), 1)
        first = row - pos_ref[rows, :]
        s = jnp.where((col <= row) & (col >= first), s, -jnp.inf)
        e = jnp.exp(s - jnp.max(s, axis=-1, keepdims=True))
        p = (e / jnp.sum(e, axis=-1, keepdims=True)).astype(BF)
        p_ref[0, rows, :n] = p
        att_ref[rows, :] = dot(p, v_ref[:n, :]).astype(BF)


def attend(queries, keys, values, positions):
    length, width = queries.shape
    heads = width // HD
    head = pl.BlockSpec((length, HD), lambda h: (0, h))
    return pl.pallas_call(
        attend_kernel,
        grid=(heads,),
        in_specs=[pl.BlockSpec((length, 1), lambda h: (0, 0)), head, head, head],
        out_specs=[head, pl.BlockSpec((1, length, length), lambda h: (h, 0, 0))],
        out_shape=[
            jax.ShapeDtypeStruct((length, width), BF),
            jax.ShapeDtypeStruct((heads, length, length), BF),
        ],
        compiler_params=pltpu.CompilerParams(vmem_limit_bytes=32 << 20),
        name="attend",
    )(positions[:, None], queries, keys, values)


def attend_back_kernel(p_ref, q_ref, k_ref, v_ref, att_ref, ga_ref, dq_ref, dk_ref, dv_ref):
    length = q_ref.shape[0]
    dk = dv = None
    for i in reversed(range(length // QB)):
        rows = slice(i * QB, (i + 1) * QB)
        n = (i + 1) * QB
        p = p_ref[0, rows, :n]
        ga = ga_ref[rows, :]
        delta = jnp.sum(
            ga.astype(F32) * att_ref[rows, :].astype(F32), axis=-1, keepdims=True
        )
        gp = dot(ga, v_ref[:n, :], NT)
        ds = ((1.0 / math.sqrt(HD)) * p.astype(F32) * (gp - delta)).astype(BF)
        dq_ref[rows, :] = dot(ds, k_ref[:n, :]).astype(BF)
        dk_i = dot(ds, q_ref[rows, :], TN)
        dv_i = dot(p, ga, TN)
        if dk is None:
            dk, dv = dk_i, dv_i
        else:
            dk_ref[n:, :] = dk[n:].astype(BF)
            dv_ref[n:, :] = dv[n:].astype(BF)
            dk, dv = dk[:n] + dk_i, dv[:n] + dv_i
    n = dk.shape[0]
    dk_ref[:n, :] = dk.astype(BF)
    dv_ref[:n, :] = dv.astype(BF)


def attend_back(probabilities, queries, keys, values, attended, grad_attended):
    length, width = queries.shape
    heads = width // HD
    head = pl.BlockSpec((length, HD), lambda h: (0, h))
    out = jax.ShapeDtypeStruct((length, width), BF)
    return pl.pallas_call(
        attend_back_kernel,
        grid=(heads,),
        in_specs=[pl.BlockSpec((1, length, length), lambda h: (h, 0, 0))] + [head] * 5,
        out_specs=[head] * 3,
        out_shape=[out] * 3,
        compiler_params=pltpu.CompilerParams(vmem_limit_bytes=32 << 20),
        name="attend_back",
    )(probabilities, queries, keys, values, attended, grad_attended)


def move(x, dy=0, dz=0, dx=0, dc=0):
    pairs = []
    for y in range(NY):
        for z in range(NZ):
            for a in range(NX):
                for c in range(NC):
                    src = ((y * NZ + z) * NX + a) * NC + c
                    dst = (
                        ((y + dy) % NY * NZ + (z + dz) % NZ) * NX + (a + dx) % NX
                    ) * NC + (c + dc) % NC
                    pairs.append((src, dst))
    return lax.ppermute(x, "blk", pairs)


def pick(x, index, axis):
    return lax.dynamic_index_in_dim(x, index, axis, keepdims=False)


def gather_ring(x, step, n, me):
    ahead = [x] + [step(x, -d) for d in range(1, n)]
    twice = jnp.stack(ahead + ahead)
    return lax.dynamic_slice_in_dim(twice, (n - me) % n, n, 0)


def reduce_ring(x, axis, step, n, me):
    got = [step(pick(x, (me + d) % n, axis), d) for d in range(1, n)]
    total = pick(x, me, axis).astype(F32)
    for g in got:
        total = total + g.astype(F32)
    return total


def y_step(x, d):
    return move(x, dy=d)


def z_step(x, d):
    return move(x, dz=d)


def gather_weight(weight, y, z, a, c):
    rows, width = weight.shape
    half = width // 2
    mine = lax.dynamic_slice_in_dim(weight, c * half, half, 1)
    other = lax.dynamic_slice_in_dim(weight, (1 - c) * half, half, 1)
    from_a = move(mine, dx=1)
    from_c = move(other, dc=1)
    from_ac = move(other, dx=1, dc=1)
    here = jnp.where(c == 0, jnp.stack([mine, from_c]), jnp.stack([from_c, mine]))
    there = jnp.where(c == 0, jnp.stack([from_a, from_ac]), jnp.stack([from_ac, from_a]))
    block = jnp.where(a == 0, jnp.concatenate([here, there]), jnp.concatenate([there, here]))
    block = block.reshape(4 * rows, half)
    part_a = gather_ring(block[:, :CUT], z_step, NZ, z).reshape(NZ * 4 * rows, CUT)
    part_a = gather_ring(part_a, y_step, NY, y).reshape(NY * NZ * 4 * rows, CUT)
    part_b = gather_ring(block[:, CUT:], y_step, NY, y)
    part_b = gather_ring(part_b, z_step, NZ, z)
    part_b = part_b.transpose(1, 0, 2, 3).reshape(NY * NZ * 4 * rows, half - CUT)
    return jnp.concatenate([part_a, part_b], axis=1)


def reduce_weight_grad(cot, att_c, att_o, y, z, a, c):
    send = dot(cot, att_o, TN).astype(BF)
    got = move(send, dc=1)
    g = (dot(cot, att_c, TN) + got.astype(F32)).astype(BF)
    features, half = g.shape
    rows = features // (NY * NZ * 4)
    g = g.reshape(NY, NZ, 4 * rows, half)
    part_a = reduce_ring(g[..., :CUT], 0, y_step, NY, y).astype(BF)
    part_a = reduce_ring(part_a, 0, z_step, NZ, z)
    part_b = reduce_ring(g[..., CUT:], 1, z_step, NZ, z).astype(BF)
    part_b = reduce_ring(part_b, 0, y_step, NY, y)
    r = jnp.concatenate([part_a, part_b], axis=1).reshape(NX, NC, rows, half)

    def of(da, dc):
        return pick(pick(r, (a + da) % NX, 0), (c + dc) % NC, 0)

    same = of(0, 0) + move(of(1, 0).astype(BF), dx=1).astype(F32)
    cross = move(of(0, 1).astype(BF), dc=1).astype(F32) + move(
        of(1, 1).astype(BF), dx=1, dc=1
    ).astype(F32)
    return jnp.where(
        c == 0,
        jnp.concatenate([same, cross], axis=1),
        jnp.concatenate([cross, same], axis=1),
    )


def per_device(queries, keys, values, positions, out_weight, cotangent):
    blk = lax.axis_index("blk")
    tp = lax.axis_index("tp")
    c = blk % NC
    a = blk // NC % NX
    z = blk // (NC * NX) % NZ
    y = blk // (NC * NX * NZ)
    width = queries.shape[1]
    half = width // 2

    def swap(x):
        return lax.ppermute(x, "tp", [(0, 1), (1, 0)])

    cot_other = swap(cotangent)
    weight_c = gather_weight(out_weight, y, z, a, c)
    weight_o = move(weight_c, dc=1)
    attended, probabilities = attend(queries, keys, values, positions)
    cot = jnp.where(
        tp == 0,
        jnp.concatenate([cotangent, cot_other], axis=1),
        jnp.concatenate([cot_other, cotangent], axis=1),
    )
    att_c = lax.dynamic_slice_in_dim(attended, c * half, half, 1)
    att_o = lax.dynamic_slice_in_dim(attended, (1 - c) * half, half, 1)
    weight_grad = reduce_weight_grad(cot, att_c, att_o, y, z, a, c)

    def partial(which):
        wc = lax.dynamic_slice_in_dim(weight_c, which * width, width, 0)
        wo = lax.dynamic_slice_in_dim(weight_o, which * width, width, 0)
        return dot(att_c, wc, NT) + dot(att_o, wo, NT)

    got = swap(partial(1 - tp).astype(BF))
    projected = (partial(tp) + got.astype(F32)).astype(BF)
    ga_c = dot(cot, weight_c).astype(BF)
    ga_o = dot(cot, weight_o).astype(BF)
    grad_attended = jnp.where(
        c == 0,
        jnp.concatenate([ga_c, ga_o], axis=1),
        jnp.concatenate([ga_o, ga_c], axis=1),
    )
    grad_queries, grad_keys, grad_values = attend_back(
        probabilities, queries, keys, values, attended, grad_attended
    )
    return (projected, weight_grad, grad_queries, grad_keys, grad_values)


def solution(mesh):
    spec = P("blk", "tp")
    return jax.shard_map(
        per_device,
        mesh=mesh,
        in_specs=(spec, spec, spec, P("blk"), spec, spec),
        out_specs=(spec,) * 5,
        check_vma=False,
    )
```

```python
import functools
import math

import jax
import jax.numpy as jnp
from jax import lax
from jax.experimental import pallas as pl
from jax.experimental.pallas import tpu as pltpu
from jax.sharding import PartitionSpec as P

HD = 128
NY, NZ, NX, NC = 4, 8, 2, 2
BF = jnp.bfloat16
F32 = jnp.float32
NT = (((1,), (1,)), ((), ()))
TN = (((0,), (0,)), ((), ()))
CUT = 384
QB = 256


def dot(a, b, dims=(((1,), (0,)), ((), ()))):
    return lax.dot_general(a, b, dims, preferred_element_type=F32)


def attend_kernel(first_ref, pos_ref, q_ref, k_ref, v_ref, att_ref, p_ref):
    length = q_ref.shape[0]
    for i in range(length // QB):
        rows = slice(i * QB, (i + 1) * QB)
        n = (i + 1) * QB
        s = dot(q_ref[rows, :], k_ref[:n, :], NT) * (1.0 / math.sqrt(HD))
        row = lax.broadcasted_iota(jnp.int32, (QB, n), 0) + i * QB
        col = lax.broadcasted_iota(jnp.int32, (QB, n), 1)
        first = row - pos_ref[rows, :]
        s = jnp.where((col <= row) & (col >= first), s, -jnp.inf)
        e = jnp.exp(s - jnp.max(s, axis=-1, keepdims=True))
        p = (e / jnp.sum(e, axis=-1, keepdims=True)).astype(BF)
        p_ref[0, rows, :n] = p
        att_ref[rows, :] = dot(p, v_ref[:n, :]).astype(BF)


def head_specs(length, heads):
    plain = pl.BlockSpec((length, HD), lambda h, first: (0, (first[0] + h) % heads))
    turned = pl.BlockSpec((length, HD), lambda h, first: (0, h))
    square = pl.BlockSpec((1, length, length), lambda h, first: (h, 0, 0))
    return plain, turned, square


def attend(first, queries, keys, values, positions):
    length, width = queries.shape
    heads = width // HD
    plain, turned, square = head_specs(length, heads)
    return pl.pallas_call(
        attend_kernel,
        grid_spec=pltpu.PrefetchScalarGridSpec(
            num_scalar_prefetch=1,
            grid=(heads,),
            in_specs=[pl.BlockSpec((length, 1), lambda h, first: (0, 0))] + [plain] * 3,
            out_specs=[turned, square],
        ),
        out_shape=[
            jax.ShapeDtypeStruct((length, width), BF),
            jax.ShapeDtypeStruct((heads, length, length), BF),
        ],
        compiler_params=pltpu.CompilerParams(vmem_limit_bytes=32 << 20),
        name="attend",
    )(first, positions, queries, keys, values)


def attend_back_kernel(first_ref, p_ref, q_ref, k_ref, v_ref, att_ref, ga_ref, *refs):
    dq_ref, dk_ref, dv_ref = refs[-3:]
    length = q_ref.shape[0]
    dk = dv = None
    for i in reversed(range(length // QB)):
        rows = slice(i * QB, (i + 1) * QB)
        n = (i + 1) * QB
        p = p_ref[0, rows, :n]
        ga = ga_ref[rows, :]
        delta = jnp.sum(
            ga.astype(F32) * att_ref[rows, :].astype(F32), axis=-1, keepdims=True
        )
        gp = dot(ga, v_ref[:n, :], NT)
        ds = ((1.0 / math.sqrt(HD)) * p.astype(F32) * (gp - delta)).astype(BF)
        dq_ref[rows, :] = dot(ds, k_ref[:n, :]).astype(BF)
        dk_i = dot(ds, q_ref[rows, :], TN)
        dv_i = dot(p, ga, TN)
        if dk is None:
            dk, dv = dk_i, dv_i
        else:
            dk_ref[n:, :] = dk[n:].astype(BF)
            dv_ref[n:, :] = dv[n:].astype(BF)
            dk, dv = dk[:n] + dk_i, dv[:n] + dv_i
    n = dk.shape[0]
    dk_ref[:n, :] = dk.astype(BF)
    dv_ref[:n, :] = dv.astype(BF)


def attend_back(first, part, probabilities, queries, keys, values, attended, grad_attended, into=()):
    length, width = queries.shape
    heads = width // HD
    n = heads // 2
    plain = pl.BlockSpec((length, HD), lambda h, first: (0, (first[0] + part * n + h) % heads))
    turned = pl.BlockSpec((length, HD), lambda h, first: (0, part * n + h))
    of_part = pl.BlockSpec((length, HD), lambda h, first: (0, h))
    square = pl.BlockSpec((1, length, length), lambda h, first: (part * n + h, 0, 0))
    out = jax.ShapeDtypeStruct((length, width), BF)
    return pl.pallas_call(
        attend_back_kernel,
        grid_spec=pltpu.PrefetchScalarGridSpec(
            num_scalar_prefetch=1,
            grid=(n,),
            in_specs=[square] + [plain] * 3 + [turned, of_part]
            + [pl.BlockSpec(memory_space=pl.ANY)] * len(into),
            out_specs=[plain] * 3,
        ),
        out_shape=[out] * 3,
        input_output_aliases={7 + k: k for k in range(len(into))},
        compiler_params=pltpu.CompilerParams(vmem_limit_bytes=32 << 20),
        name="attend_back",
    )(first, probabilities, queries, keys, values, attended, grad_attended, *into)


def move(x, dy=0, dz=0, dx=0, dc=0):
    pairs = []
    for y in range(NY):
        for z in range(NZ):
            for a in range(NX):
                for c in range(NC):
                    src = ((y * NZ + z) * NX + a) * NC + c
                    dst = (
                        ((y + dy) % NY * NZ + (z + dz) % NZ) * NX + (a + dx) % NX
                    ) * NC + (c + dc) % NC
                    pairs.append((src, dst))
    return lax.ppermute(x, "blk", pairs)


def pick(x, index, axis):
    return lax.dynamic_index_in_dim(x, index, axis, keepdims=False)


def put(buffer, block, index, axis):
    return lax.dynamic_update_index_in_dim(buffer, block, index, axis)


def y_step(x, d):
    return move(x, dy=d)


def z_step(x, d):
    return move(x, dz=d)


def tie(x, *others):
    return lax.optimization_barrier((x,) + others)[0]


def gather_ring(x, step, n, at, axis, cut, beside=()):
    split, join = cut
    beside = list(beside) + [None] * n
    shape = x.shape[:axis] + (n,) + x.shape[axis:]
    out = jnp.broadcast_to(jnp.expand_dims(x, axis), shape)
    up = down = x
    for d in range(1, n // 2 + 1):
        work = beside[d - 1](up, down) if beside[d - 1] else ()
        if d == n // 2:
            far = join(step(split(up)[0], 1), step(split(down)[1], -1))
            out = put(out, far, at(d), axis)
            return tie(out, *work)
        up, down = step(up, 1), step(down, -1)
        out = put(out, up, at(-d), axis)
        out = put(out, down, at(d), axis)
        up, down = lax.optimization_barrier((up, down) + tuple(work))[:2]


def reduce_ring(x, axis, step, n, at, cut, beside=()):
    split, join = cut
    beside = list(beside) + [None] * n

    def block(d):
        return pick(x, at(d), axis)

    def add(u, w):
        return (u.astype(F32) + w.astype(F32)).astype(x.dtype)

    up, down = split(block(n // 2))
    for k, d in enumerate(range(n // 2, -1, -1)):
        if 0 < d < n // 2:
            up_block, down_block = block(d), block(-d)
            if d == n // 2 - 1:
                u, w = split(up_block)
                up_block = join(add(u, up), w)
                u, w = split(down_block)
                down_block = join(u, add(w, down))
            else:
                up_block, down_block = add(up_block, up), add(down_block, down)
            up, down = up_block, down_block
        elif d == 0:
            return block(0).astype(F32) + up.astype(F32) + down.astype(F32)
        work = beside[k](up, down) if beside[k] else ()
        up, down = step(up, 1), step(down, -1)
        if work:
            up, down = lax.optimization_barrier((up, down) + tuple(work))[:2]


def columns(at):
    return (
        lambda x: (x[..., :at], x[..., at:]),
        lambda u, w: jnp.concatenate([u, w], axis=-1),
    )


def rows(at):
    return lambda x: (x[:at], x[at:]), lambda u, w: jnp.concatenate([u, w], axis=0)


def gather_chips(weight, a, c):
    shard, width = weight.shape
    half = width // 2
    mine = lax.dynamic_slice_in_dim(weight, c * half, half, 1)
    other = lax.dynamic_slice_in_dim(weight, (1 - c) * half, half, 1)
    from_a = move(mine, dx=1)
    from_c = move(other, dc=1)
    from_ac = move(other, dx=1, dc=1)
    here = jnp.where(c == 0, jnp.stack([mine, from_c]), jnp.stack([from_c, mine]))
    there = jnp.where(c == 0, jnp.stack([from_a, from_ac]), jnp.stack([from_ac, from_a]))
    block = jnp.where(a == 0, jnp.concatenate([here, there]), jnp.concatenate([there, here]))
    return block.reshape(NX * NC * shard, half)


def reduce_chips(r, a, c):
    def of(da, dc):
        return pick(pick(r, (a + da) % NX, 0), (c + dc) % NC, 0)

    same = of(0, 0) + move(of(1, 0).astype(BF), dx=1).astype(F32)
    cross = move(of(0, 1).astype(BF), dc=1).astype(F32) + move(
        of(1, 1).astype(BF), dx=1, dc=1
    ).astype(F32)
    return jnp.where(
        c == 0,
        jnp.concatenate([same, cross], axis=1),
        jnp.concatenate([cross, same], axis=1),
    )


def per_device(queries, keys, values, positions, out_weight, cotangent):
    blk = lax.axis_index("blk")
    tp = lax.axis_index("tp")
    c = blk % NC
    a = blk // NC % NX
    z = blk // (NC * NX) % NZ
    y = blk // (NC * NX * NZ)
    width = queries.shape[1]
    half = width // 2
    shard = out_weight.shape[0]
    positions = positions[:, None]
    first = (c * (half // HD)).astype(jnp.int32)[None]

    def at_y(d):
        to = (y + d) % NY
        return (to // 2 + tp) % 2 * 2 + to % 2

    def at_z(d):
        return (z + d) % NZ

    def swap(x):
        return lax.ppermute(x, "tp", [(0, 1), (1, 0)])

    cot_other = swap(cotangent)
    done = {}

    def forward(up, down):
        pos = tie(positions, up, down)
        done["att"], done["p"] = attend(first, queries, keys, values, pos)
        return (done["att"],)

    def grad(up, down):
        att_c, att_o = done["att"][:, :half], done["att"][:, half:]
        cot = tie(cotangent, up, down)
        own_o = dot(cot, att_o, TN).astype(BF)
        own_c = dot(cot, att_c, TN).astype(BF)
        other_o = dot(tie(cot_other, own_o, own_c), att_o, TN).astype(BF)
        sent = jnp.concatenate([own_o, other_o], axis=0)
        done["got"] = move(sent, dc=1)
        other_c = dot(tie(cot_other, sent), att_c, TN).astype(BF)
        done["g"] = jnp.concatenate([own_c, other_c], axis=0)
        return (other_c,)

    def grad_sum(up, down):
        got = tie(done["got"], up, down)
        done["g"] = (done["g"].astype(F32) + got.astype(F32)).astype(BF)
        return (done["g"],)

    block = gather_chips(out_weight, a, c)
    block = gather_ring(block, y_step, NY, at_y, 0, columns(CUT))
    weight_c = gather_ring(
        block, z_step, NZ, at_z, 1, rows(NY // 2), [forward, grad, grad_sum]
    ).reshape(2 * width, half)
    att = done["att"]
    att_c, att_o = att[:, :half], att[:, half:]
    cot = jnp.concatenate([cotangent, cot_other], axis=1)

    def back(part, grad_attended, into=()):
        done["grads"] = attend_back(
            first, part, done["p"], queries, keys, values, att, grad_attended, into
        )
        return tuple(done["grads"])

    def after_gather(up, down):
        done["weight_o"] = move(tie(weight_c, up, down), dc=1)
        wc = tie(weight_c, up, down)
        ga = dot(cot, wc).astype(BF)
        partial = dot(att_c, wc[width:], NT) + dot(att_o, done["weight_o"][width:], NT)
        done["got"] = swap(partial.astype(BF))
        done["partial"] = partial
        return back(0, tie(ga, partial))

    def grad_attended_o(up, down):
        done["ga_o"] = dot(cot, tie(done["weight_o"], up, down)).astype(BF)
        return (done["ga_o"],)

    def back_o(up, down):
        return back(1, tie(done["ga_o"], up, down), done["grads"])

    def project_own(up, down):
        wc = tie(weight_c, up, down)
        done["own"] = dot(att_c, wc[:width], NT) + dot(att_o, done["weight_o"][:width], NT)
        return (done["own"],)

    g = done["g"].reshape(NY, NZ, NX * NC * shard, half)
    g = reduce_ring(g, 0, y_step, NY, at_y, rows(NZ // 2), [None, after_gather]).astype(BF)
    r = reduce_ring(
        g, 0, z_step, NZ, at_z, columns(CUT), [grad_attended_o, back_o, project_own]
    )
    weight_grad = reduce_chips(r.reshape(NX, NC, shard, half), a, c)
    projected = (done["own"] + done["got"].astype(F32)).astype(BF)
    return (projected, weight_grad, *done["grads"])


def solution(mesh):
    spec = P("blk", "tp")
    return jax.shard_map(
        per_device,
        mesh=mesh,
        in_specs=(spec, spec, spec, P("blk"), spec, spec),
        out_specs=(spec,) * 5,
        check_vma=False,
    )
```

```python
import functools
import math

import jax
import jax.numpy as jnp
from jax import lax
from jax.experimental import pallas as pl
from jax.experimental.pallas import tpu as pltpu
from jax.sharding import PartitionSpec as P

HD = 128
NY, NZ, NX, NC = 4, 8, 2, 2
BF = jnp.bfloat16
F32 = jnp.float32
NT = (((1,), (1,)), ((), ()))
TN = (((0,), (0,)), ((), ()))
CUT = 384
QB = 256


def dot(a, b, dims=(((1,), (0,)), ((), ()))):
    return lax.dot_general(a, b, dims, preferred_element_type=F32)


def attend_kernel(first_ref, pos_ref, q_ref, k_ref, v_ref, att_ref, p_ref):
    length = q_ref.shape[0]
    for i in range(length // QB):
        rows = slice(i * QB, (i + 1) * QB)
        n = (i + 1) * QB
        s = dot(q_ref[rows, :], k_ref[:n, :], NT)
        row = lax.broadcasted_iota(jnp.int32, (QB, n), 0) + i * QB
        col = lax.broadcasted_iota(jnp.int32, (QB, n), 1)
        first = row - pos_ref[rows, :]
        s = jnp.where((col <= row) & (col >= first), s, -jnp.inf)
        e = jnp.exp((s - jnp.max(s, axis=-1, keepdims=True)) * (1.0 / math.sqrt(HD)))
        p = (e * (1.0 / jnp.sum(e, axis=-1, keepdims=True))).astype(BF)
        p_ref[0, rows, :n] = p
        att_ref[rows, :] = dot(p, v_ref[:n, :]).astype(BF)


def head_specs(length, heads):
    plain = pl.BlockSpec((length, HD), lambda h, first: (0, (first[0] + h) % heads))
    turned = pl.BlockSpec((length, HD), lambda h, first: (0, h))
    square = pl.BlockSpec((1, length, length), lambda h, first: (h, 0, 0))
    return plain, turned, square


def attend(first, queries, keys, values, positions):
    length, width = queries.shape
    heads = width // HD
    plain, turned, square = head_specs(length, heads)
    return pl.pallas_call(
        attend_kernel,
        grid_spec=pltpu.PrefetchScalarGridSpec(
            num_scalar_prefetch=1,
            grid=(heads,),
            in_specs=[pl.BlockSpec((length, 1), lambda h, first: (0, 0))] + [plain] * 3,
            out_specs=[turned, square],
        ),
        out_shape=[
            jax.ShapeDtypeStruct((length, width), BF),
            jax.ShapeDtypeStruct((heads, length, length), BF),
        ],
        compiler_params=pltpu.CompilerParams(vmem_limit_bytes=32 << 20),
        name="attend",
    )(first, positions, queries, keys, values)


def attend_back_kernel(first_ref, p_ref, q_ref, k_ref, v_ref, att_ref, ga_ref, *refs):
    dq_ref, dk_ref, dv_ref = refs[-3:]
    length = q_ref.shape[0]
    dk = dv = None
    for i in reversed(range(length // QB)):
        rows = slice(i * QB, (i + 1) * QB)
        n = (i + 1) * QB
        p = p_ref[0, rows, :n]
        ga = ga_ref[rows, :]
        delta = jnp.sum(
            ga.astype(F32) * att_ref[rows, :].astype(F32), axis=-1, keepdims=True
        )
        gp = dot(ga, v_ref[:n, :], NT)
        ds = ((1.0 / math.sqrt(HD)) * p.astype(F32) * (gp - delta)).astype(BF)
        dq_ref[rows, :] = dot(ds, k_ref[:n, :]).astype(BF)
        dk_i = dot(ds, q_ref[rows, :], TN)
        dv_i = dot(p, ga, TN)
        if dk is None:
            dk, dv = dk_i, dv_i
        else:
            dk_ref[n:, :] = dk[n:].astype(BF)
            dv_ref[n:, :] = dv[n:].astype(BF)
            dk, dv = dk[:n] + dk_i, dv[:n] + dv_i
    n = dk.shape[0]
    dk_ref[:n, :] = dk.astype(BF)
    dv_ref[:n, :] = dv.astype(BF)


def attend_back(first, part, probabilities, queries, keys, values, attended, grad_attended, into=()):
    length, width = queries.shape
    heads = width // HD
    n = heads // 2
    plain = pl.BlockSpec((length, HD), lambda h, first: (0, (first[0] + part * n + h) % heads))
    turned = pl.BlockSpec((length, HD), lambda h, first: (0, part * n + h))
    of_part = pl.BlockSpec((length, HD), lambda h, first: (0, h))
    square = pl.BlockSpec((1, length, length), lambda h, first: (part * n + h, 0, 0))
    out = jax.ShapeDtypeStruct((length, width), BF)
    return pl.pallas_call(
        attend_back_kernel,
        grid_spec=pltpu.PrefetchScalarGridSpec(
            num_scalar_prefetch=1,
            grid=(n,),
            in_specs=[square] + [plain] * 3 + [turned, of_part]
            + [pl.BlockSpec(memory_space=pl.ANY)] * len(into),
            out_specs=[plain] * 3,
        ),
        out_shape=[out] * 3,
        input_output_aliases={7 + k: k for k in range(len(into))},
        compiler_params=pltpu.CompilerParams(vmem_limit_bytes=32 << 20),
        name="attend_back",
    )(first, probabilities, queries, keys, values, attended, grad_attended, *into)


FB = 256


def grad_attended_half(cot_own, cot_other, weight):
    length, width = cot_own.shape
    half = weight.shape[1]
    n = width // half

    def kernel(own_ref, other_ref, w_ref, out_ref, acc_ref):
        i = pl.program_id(0)

        @pl.when(i == 0)
        def _():
            acc_ref[...] = dot(own_ref[...], w_ref[...])

        @pl.when((i > 0) & (i < n))
        def _():
            acc_ref[...] += dot(own_ref[...], w_ref[...])

        @pl.when((i >= n) & (i < 2 * n - 1))
        def _():
            acc_ref[...] += dot(other_ref[...], w_ref[...])

        @pl.when(i == 2 * n - 1)
        def _():
            out_ref[...] = (acc_ref[...] + dot(other_ref[...], w_ref[...])).astype(BF)

    return pl.pallas_call(
        kernel,
        grid=(2 * n,),
        in_specs=[
            pl.BlockSpec((length, half), lambda i: (0, jnp.minimum(i, n - 1))),
            pl.BlockSpec((length, half), lambda i: (0, jnp.maximum(i - n, 0))),
            pl.BlockSpec((half, half), lambda i: (i, 0)),
        ],
        out_specs=pl.BlockSpec((length, half), lambda i: (0, 0)),
        out_shape=jax.ShapeDtypeStruct((length, half), BF),
        scratch_shapes=[pltpu.VMEM((length, half), F32)],
        compiler_params=pltpu.CompilerParams(vmem_limit_bytes=32 << 20),
        name="grad_attended_half",
    )(cot_own, cot_other, weight)


def project(att, weight_c, weight_o, side, got=None):
    length, width = att.shape
    half = width // 2
    n = width // FB

    def kernel(att_ref, wc_ref, wo_ref, *refs):
        p = dot(att_ref[:, :half], wc_ref[...], NT) + dot(att_ref[:, half:], wo_ref[...], NT)
        if got is not None:
            p = p + refs[0][...].astype(F32)
        refs[-1][...] = p.astype(BF)

    block = pl.BlockSpec((length, FB), lambda i: (0, i))
    rows_of = pl.BlockSpec((FB, half), lambda i: (side * n + i, 0))
    more = [] if got is None else [got]
    return pl.pallas_call(
        kernel,
        grid=(n,),
        in_specs=[pl.BlockSpec((length, width), lambda i: (0, 0)), rows_of, rows_of]
        + [block] * len(more),
        out_specs=block,
        out_shape=jax.ShapeDtypeStruct((length, width), BF),
        compiler_params=pltpu.CompilerParams(vmem_limit_bytes=32 << 20),
        name="project",
    )(att, weight_c, weight_o, *more)


def move(x, dy=0, dz=0, dx=0, dc=0):
    pairs = []
    for y in range(NY):
        for z in range(NZ):
            for a in range(NX):
                for c in range(NC):
                    src = ((y * NZ + z) * NX + a) * NC + c
                    dst = (
                        ((y + dy) % NY * NZ + (z + dz) % NZ) * NX + (a + dx) % NX
                    ) * NC + (c + dc) % NC
                    pairs.append((src, dst))
    return lax.ppermute(x, "blk", pairs)


def pick(x, index, axis):
    return lax.dynamic_index_in_dim(x, index, axis, keepdims=False)


def put(buffer, block, index, axis):
    return lax.dynamic_update_index_in_dim(buffer, block, index, axis)


def y_step(x, d):
    return move(x, dy=d)


def z_step(x, d):
    return move(x, dz=d)


def tie(x, *others):
    return lax.optimization_barrier((x,) + others)[0]


def assemble(blocks, places, n):
    *whole, first, last = blocks
    k = whole[0].shape[0]

    def kernel(place_ref, *refs):
        *block_refs, first_ref, last_ref, out_ref = refs
        for i, ref in enumerate(block_refs):
            out_ref[:, place_ref[i]] = ref[...]
        at = place_ref[n - 1]
        out_ref[: k // 2, at] = first_ref[...]
        out_ref[k // 2 :, at] = last_ref[...]

    vmem = pl.BlockSpec(memory_space=pltpu.VMEM)
    return pl.pallas_call(
        kernel,
        in_specs=[pl.BlockSpec(memory_space=pltpu.SMEM)] + [vmem] * len(blocks),
        out_specs=vmem,
        out_shape=jax.ShapeDtypeStruct((k, n) + whole[0].shape[1:], whole[0].dtype),
        compiler_params=pltpu.CompilerParams(vmem_limit_bytes=32 << 20),
        name="assemble",
    )(jnp.stack(places).astype(jnp.int32), *blocks)


def gather_ring(x, step, n, at, beside):
    blocks, places = [x], [at(0)]
    up = down = x
    for d in range(1, n // 2):
        work = beside[d - 1](up, down)
        up, down = step(up, 1), step(down, -1)
        blocks += [up, down]
        places += [at(-d), at(d)]
        up, down = lax.optimization_barrier((up, down) + tuple(work))[:2]
    k = x.shape[0] // 2
    return blocks + [step(up[:k], 1), step(down[k:], -1)], places + [at(n // 2)]


def gather_direct(x, step, n, at, axis):
    shape = x.shape[:axis] + (n,) + x.shape[axis:]
    out = jnp.broadcast_to(jnp.expand_dims(x, axis), shape)
    for d in range(1, n):
        out = put(out, step(x, d), at(-d), axis)
    return out


def reduce_ring(x, axis, step, n, at, cut):
    split, join = cut

    def block(d):
        return pick(x, at(d), axis)

    def add(u, w):
        return (u.astype(F32) + w.astype(F32)).astype(x.dtype)

    up, down = split(block(n // 2))
    for d in range(n // 2 - 1, -1, -1):
        beside = yield up, down
        up, down = step(up, 1), step(down, -1)
        if beside:
            up, down = lax.optimization_barrier((up, down) + tuple(beside))[:2]
        if d == 0:
            yield block(0).astype(F32) + up.astype(F32) + down.astype(F32)
        elif d == n // 2 - 1:
            u, w = split(block(d))
            v, t = split(block(-d))
            up, down = join(add(u, up), w), join(v, add(t, down))
        else:
            up, down = add(block(d), up), add(block(-d), down)


def columns(at):
    return (
        lambda x: (x[..., :at], x[..., at:]),
        lambda u, w: jnp.concatenate([u, w], axis=-1),
    )


def rows(at):
    return lambda x: (x[:at], x[at:]), lambda u, w: jnp.concatenate([u, w], axis=0)


def gather_chips(weight, a, c):
    shard, width = weight.shape
    half = width // 2
    mine = lax.dynamic_slice_in_dim(weight, c * half, half, 1)
    other = lax.dynamic_slice_in_dim(weight, (1 - c) * half, half, 1)
    from_a = move(mine, dx=1)
    from_c = move(other, dc=1)
    from_ac = move(other, dx=1, dc=1)
    here = jnp.where(c == 0, jnp.stack([mine, from_c]), jnp.stack([from_c, mine]))
    there = jnp.where(c == 0, jnp.stack([from_a, from_ac]), jnp.stack([from_ac, from_a]))
    block = jnp.where(a == 0, jnp.concatenate([here, there]), jnp.concatenate([there, here]))
    return block.reshape(NX * NC * shard, half)


def reduce_chips(r, a, c):
    def of(da, dc):
        return pick(pick(r, (a + da) % NX, 0), (c + dc) % NC, 0)

    same = of(0, 0) + move(of(1, 0).astype(BF), dx=1).astype(F32)
    cross = move(of(0, 1).astype(BF), dc=1).astype(F32) + move(
        of(1, 1).astype(BF), dx=1, dc=1
    ).astype(F32)
    return jnp.where(
        c == 0,
        jnp.concatenate([same, cross], axis=1),
        jnp.concatenate([cross, same], axis=1),
    )


def per_device(queries, keys, values, positions, out_weight, cotangent):
    blk = lax.axis_index("blk")
    tp = lax.axis_index("tp")
    c = blk % NC
    a = blk // NC % NX
    z = blk // (NC * NX) % NZ
    y = blk // (NC * NX * NZ)
    width = queries.shape[1]
    half = width // 2
    shard = out_weight.shape[0]
    positions = positions[:, None]
    first = (c * (half // HD)).astype(jnp.int32)[None]

    def at_y(d):
        to = (y + d) % NY
        return (to // 2 + tp) % 2 * 2 + to % 2

    def at_z(d):
        return (z + d) % NZ

    def swap(x):
        return lax.ppermute(x, "tp", [(0, 1), (1, 0)])

    done = {}

    def forward(up, down):
        pos = tie(positions, up, down)
        done["att"], done["p"] = attend(first, queries, keys, values, pos)
        return (done["att"],)

    def grad_of_sibling(up, down):
        att_o = done["att"][:, half:]
        own_o = dot(tie(cotangent, up, down), att_o, TN).astype(BF)
        other_o = dot(tie(cot_other, up, down), att_o, TN).astype(BF)
        done["sent"] = jnp.concatenate([own_o, other_o], axis=0)
        return (done["sent"],)

    def grad_of_core(up, down):
        att_c = done["att"][:, :half]
        done["got"] = move(tie(done["sent"], up, down), dc=1)
        own_c = dot(tie(cotangent, up, down), att_c, TN).astype(BF)
        other_c = dot(tie(cot_other, up, down), att_c, TN).astype(BF)
        g = jnp.concatenate([own_c, other_c], axis=0).astype(F32)
        g = (g + done["got"].astype(F32)).astype(BF)
        done["ring"] = reduce_ring(
            g.reshape(NY, NZ, NX * NC * shard, half), 0, y_step, NY, at_y, rows(NZ // 2)
        )
        done["sends"] = next(done["ring"])
        return done["sends"]

    block = gather_chips(out_weight, a, c)
    cot_other = swap(tie(cotangent, block))
    block = gather_direct(block, y_step, NY, at_y, 0)
    blocks, places = gather_ring(
        block, z_step, NZ, at_z, [forward, grad_of_sibling, grad_of_core]
    )
    att, ring = done["att"], done["ring"]

    def back(part, grad_attended, into=()):
        return attend_back(
            first, part, done["p"], queries, keys, values, att, grad_attended, into
        )

    sends = ring.send(())
    blocks[-1] = tie(blocks[-1], *sends)
    weight_c = assemble(blocks, places, NZ).reshape(2 * width, half)
    weight_o = move(weight_c, dc=1)
    ga_c = grad_attended_half(cotangent, tie(cot_other, *sends), weight_c)
    partial = project(att, weight_c, tie(weight_o, ga_c), 1)
    got = swap(partial)
    grads = back(0, tie(ga_c, partial, *sends))
    ga_o = grad_attended_half(cotangent, tie(cot_other, *sends), tie(weight_o, partial))
    g = ring.send((*grads, ga_o)).astype(BF)

    ring = reduce_ring(g, 0, z_step, NZ, at_z, columns(CUT))
    sends = next(ring)
    grads = back(1, tie(ga_o, *sends), grads)
    sends = ring.send(tuple(grads))
    sends = ring.send(())
    projected = project(att, weight_c, weight_o, 0, tie(got, *sends))
    sends = ring.send((projected,))
    r = ring.send(())
    weight_grad = reduce_chips(r.reshape(NX, NC, shard, half), a, c)
    return (projected, weight_grad, *grads)


def solution(mesh):
    spec = P("blk", "tp")
    return jax.shard_map(
        per_device,
        mesh=mesh,
        in_specs=(spec, spec, spec, P("blk"), spec, spec),
        out_specs=(spec,) * 5,
        check_vma=False,
    )
```

```python
import functools
import math

import jax
import jax.numpy as jnp
from jax import lax
from jax.experimental import pallas as pl
from jax.experimental.pallas import tpu as pltpu
from jax.sharding import PartitionSpec as P

HD = 128
NY, NZ, NX, NC = 4, 8, 2, 2
BF = jnp.bfloat16
F32 = jnp.float32
NT = (((1,), (1,)), ((), ()))
TN = (((0,), (0,)), ((), ()))
CUT = 384
QB = 256


def dot(a, b, dims=(((1,), (0,)), ((), ()))):
    return lax.dot_general(a, b, dims, preferred_element_type=F32)


def attend_kernel(first_ref, pos_ref, q_ref, k_ref, v_ref, att_ref, p_ref):
    length = q_ref.shape[0]
    for i in range(length // QB):
        rows = slice(i * QB, (i + 1) * QB)
        n = (i + 1) * QB
        s = dot(q_ref[rows, :], k_ref[:n, :], NT)
        row = lax.broadcasted_iota(jnp.int32, (QB, n), 0) + i * QB
        col = lax.broadcasted_iota(jnp.int32, (QB, n), 1)
        first = row - pos_ref[rows, :]
        s = jnp.where((col <= row) & (col >= first), s, -jnp.inf)
        e = jnp.exp((s - jnp.max(s, axis=-1, keepdims=True)) * (1.0 / math.sqrt(HD)))
        p = (e * (1.0 / jnp.sum(e, axis=-1, keepdims=True))).astype(BF)
        p_ref[0, rows, :n] = p
        att_ref[rows, :] = dot(p, v_ref[:n, :]).astype(BF)


def head_specs(length, heads):
    plain = pl.BlockSpec((length, HD), lambda h, first: (0, (first[0] + h) % heads))
    turned = pl.BlockSpec((length, HD), lambda h, first: (0, h))
    square = pl.BlockSpec((1, length, length), lambda h, first: (h, 0, 0))
    return plain, turned, square


def attend(first, queries, keys, values, positions):
    length, width = queries.shape
    heads = width // HD
    plain, turned, square = head_specs(length, heads)
    return pl.pallas_call(
        attend_kernel,
        grid_spec=pltpu.PrefetchScalarGridSpec(
            num_scalar_prefetch=1,
            grid=(heads,),
            in_specs=[pl.BlockSpec((length, 1), lambda h, first: (0, 0))] + [plain] * 3,
            out_specs=[turned, square],
        ),
        out_shape=[
            jax.ShapeDtypeStruct((length, width), BF),
            jax.ShapeDtypeStruct((heads, length, length), BF),
        ],
        compiler_params=pltpu.CompilerParams(vmem_limit_bytes=32 << 20),
        name="attend",
    )(first, positions, queries, keys, values)


def attend_back_kernel(first_ref, p_ref, q_ref, k_ref, v_ref, att_ref, ga_ref, *refs):
    dq_ref, dk_ref, dv_ref = refs[-3:]
    length = q_ref.shape[0]
    dk = dv = None
    for i in reversed(range(length // QB)):
        rows = slice(i * QB, (i + 1) * QB)
        n = (i + 1) * QB
        p = p_ref[0, rows, :n]
        ga = ga_ref[rows, :]
        delta = jnp.sum(
            ga.astype(F32) * att_ref[rows, :].astype(F32), axis=-1, keepdims=True
        )
        gp = dot(ga, v_ref[:n, :], NT)
        ds = ((1.0 / math.sqrt(HD)) * p.astype(F32) * (gp - delta)).astype(BF)
        dq_ref[rows, :] = dot(ds, k_ref[:n, :]).astype(BF)
        dk_i = dot(ds, q_ref[rows, :], TN)
        dv_i = dot(p, ga, TN)
        if dk is None:
            dk, dv = dk_i, dv_i
        else:
            dk_ref[n:, :] = dk[n:].astype(BF)
            dv_ref[n:, :] = dv[n:].astype(BF)
            dk, dv = dk[:n] + dk_i, dv[:n] + dv_i
    n = dk.shape[0]
    dk_ref[:n, :] = dk.astype(BF)
    dv_ref[:n, :] = dv.astype(BF)


def attend_back(first, part, probabilities, queries, keys, values, attended, grad_attended, into=()):
    length, width = queries.shape
    heads = width // HD
    n = heads // 2
    plain = pl.BlockSpec((length, HD), lambda h, first: (0, (first[0] + part * n + h) % heads))
    turned = pl.BlockSpec((length, HD), lambda h, first: (0, part * n + h))
    of_part = pl.BlockSpec((length, HD), lambda h, first: (0, h))
    square = pl.BlockSpec((1, length, length), lambda h, first: (part * n + h, 0, 0))
    out = jax.ShapeDtypeStruct((length, width), BF)
    return pl.pallas_call(
        attend_back_kernel,
        grid_spec=pltpu.PrefetchScalarGridSpec(
            num_scalar_prefetch=1,
            grid=(n,),
            in_specs=[square] + [plain] * 3 + [turned, of_part]
            + [pl.BlockSpec(memory_space=pl.ANY)] * len(into),
            out_specs=[plain] * 3,
        ),
        out_shape=[out] * 3,
        input_output_aliases={7 + k: k for k in range(len(into))},
        compiler_params=pltpu.CompilerParams(vmem_limit_bytes=32 << 20),
        name="attend_back",
    )(first, probabilities, queries, keys, values, attended, grad_attended, *into)


FB = 256


def grad_attended_half(cot_own, cot_other, weight):
    length, width = cot_own.shape
    half = weight.shape[1]
    n = width // half

    def kernel(own_ref, other_ref, w_ref, out_ref, acc_ref):
        i = pl.program_id(0)

        @pl.when(i == 0)
        def _():
            acc_ref[...] = dot(own_ref[...], w_ref[...])

        @pl.when((i > 0) & (i < n))
        def _():
            acc_ref[...] += dot(own_ref[...], w_ref[...])

        @pl.when((i >= n) & (i < 2 * n - 1))
        def _():
            acc_ref[...] += dot(other_ref[...], w_ref[...])

        @pl.when(i == 2 * n - 1)
        def _():
            out_ref[...] = (acc_ref[...] + dot(other_ref[...], w_ref[...])).astype(BF)

    return pl.pallas_call(
        kernel,
        grid=(2 * n,),
        in_specs=[
            pl.BlockSpec((length, half), lambda i: (0, jnp.minimum(i, n - 1))),
            pl.BlockSpec((length, half), lambda i: (0, jnp.maximum(i - n, 0))),
            pl.BlockSpec((half, half), lambda i: (i, 0)),
        ],
        out_specs=pl.BlockSpec((length, half), lambda i: (0, 0)),
        out_shape=jax.ShapeDtypeStruct((length, half), BF),
        scratch_shapes=[pltpu.VMEM((length, half), F32)],
        compiler_params=pltpu.CompilerParams(vmem_limit_bytes=32 << 20),
        name="grad_attended_half",
    )(cot_own, cot_other, weight)


def project(att, weight_c, weight_o, side, got=None):
    length, width = att.shape
    half = width // 2
    n = width // FB

    def kernel(att_ref, wc_ref, wo_ref, *refs):
        p = dot(att_ref[:, :half], wc_ref[...], NT) + dot(att_ref[:, half:], wo_ref[...], NT)
        if got is not None:
            p = p + refs[0][...].astype(F32)
        refs[-1][...] = p.astype(BF)

    block = pl.BlockSpec((length, FB), lambda i: (0, i))
    rows_of = pl.BlockSpec((FB, half), lambda i: (side * n + i, 0))
    more = [] if got is None else [got]
    return pl.pallas_call(
        kernel,
        grid=(n,),
        in_specs=[pl.BlockSpec((length, width), lambda i: (0, 0)), rows_of, rows_of]
        + [block] * len(more),
        out_specs=block,
        out_shape=jax.ShapeDtypeStruct((length, width), BF),
        compiler_params=pltpu.CompilerParams(vmem_limit_bytes=32 << 20),
        name="project",
    )(att, weight_c, weight_o, *more)


def move(x, dy=0, dz=0, dx=0, dc=0):
    pairs = []
    for y in range(NY):
        for z in range(NZ):
            for a in range(NX):
                for c in range(NC):
                    src = ((y * NZ + z) * NX + a) * NC + c
                    dst = (
                        ((y + dy) % NY * NZ + (z + dz) % NZ) * NX + (a + dx) % NX
                    ) * NC + (c + dc) % NC
                    pairs.append((src, dst))
    return lax.ppermute(x, "blk", pairs)


def pick(x, index, axis):
    return lax.dynamic_index_in_dim(x, index, axis, keepdims=False)


def put(buffer, block, index, axis):
    return lax.dynamic_update_index_in_dim(buffer, block, index, axis)


def y_step(x, d):
    return move(x, dy=d)


def z_step(x, d):
    return move(x, dz=d)


def tie(x, *others):
    return lax.optimization_barrier((x,) + others)[0]


def assemble(blocks, places, n):
    *whole, first, last = blocks
    k = whole[0].shape[0]

    def kernel(place_ref, *refs):
        *block_refs, first_ref, last_ref, out_ref = refs
        for i, ref in enumerate(block_refs):
            out_ref[:, place_ref[i]] = ref[...]
        at = place_ref[n - 1]
        out_ref[: k // 2, at] = first_ref[...]
        out_ref[k // 2 :, at] = last_ref[...]

    vmem = pl.BlockSpec(memory_space=pltpu.VMEM)
    return pl.pallas_call(
        kernel,
        in_specs=[pl.BlockSpec(memory_space=pltpu.SMEM)] + [vmem] * len(blocks),
        out_specs=vmem,
        out_shape=jax.ShapeDtypeStruct((k, n) + whole[0].shape[1:], whole[0].dtype),
        compiler_params=pltpu.CompilerParams(vmem_limit_bytes=32 << 20),
        name="assemble",
    )(jnp.stack(places).astype(jnp.int32), *blocks)


def gather_ring(x, step, n, at, beside):
    blocks, places = [x], [at(0)]
    up = down = x
    for d in range(1, n // 2):
        work = beside[d - 1](up, down)
        up, down = step(up, 1), step(down, -1)
        blocks += [up, down]
        places += [at(-d), at(d)]
        up, down = lax.optimization_barrier((up, down) + tuple(work))[:2]
    k = x.shape[0] // 2
    return blocks + [step(up[:k], 1), step(down[k:], -1)], places + [at(n // 2)]


def gather_direct(x, step, n, at, axis):
    shape = x.shape[:axis] + (n,) + x.shape[axis:]
    out = jnp.broadcast_to(jnp.expand_dims(x, axis), shape)
    for d in range(1, n):
        out = put(out, step(x, d), at(-d), axis)
    return out


def reduce_ring(x, axis, step, n, at, cut):
    split, join = cut

    def block(d):
        return pick(x, at(d), axis)

    def add(u, w):
        return (u.astype(F32) + w.astype(F32)).astype(x.dtype)

    up, down = split(block(n // 2))
    for d in range(n // 2 - 1, -1, -1):
        beside = yield up, down
        up, down = step(up, 1), step(down, -1)
        if beside:
            up, down = lax.optimization_barrier((up, down) + tuple(beside))[:2]
        if d == 0:
            yield block(0).astype(F32) + up.astype(F32) + down.astype(F32)
        elif d == n // 2 - 1:
            u, w = split(block(d))
            v, t = split(block(-d))
            up, down = join(add(u, up), w), join(v, add(t, down))
        else:
            up, down = add(block(d), up), add(block(-d), down)


def columns(at):
    return (
        lambda x: (x[..., :at], x[..., at:]),
        lambda u, w: jnp.concatenate([u, w], axis=-1),
    )


def rows(at):
    return lambda x: (x[:at], x[at:]), lambda u, w: jnp.concatenate([u, w], axis=0)


def gather_chips(weight, a, c):
    shard, width = weight.shape
    half = width // 2
    mine = lax.dynamic_slice_in_dim(weight, c * half, half, 1)
    other = lax.dynamic_slice_in_dim(weight, (1 - c) * half, half, 1)
    from_a = move(mine, dx=1)
    from_c = move(other, dc=1)
    from_ac = move(other, dx=1, dc=1)
    here = jnp.where(c == 0, jnp.stack([mine, from_c]), jnp.stack([from_c, mine]))
    there = jnp.where(c == 0, jnp.stack([from_a, from_ac]), jnp.stack([from_ac, from_a]))
    block = jnp.where(a == 0, jnp.concatenate([here, there]), jnp.concatenate([there, here]))
    return block.reshape(NX * NC * shard, half)


def reduce_chips(r, a, c):
    def of(da, dc):
        return pick(pick(r, (a + da) % NX, 0), (c + dc) % NC, 0)

    same = of(0, 0) + move(of(1, 0).astype(BF), dx=1).astype(F32)
    cross = move(of(0, 1).astype(BF), dc=1).astype(F32) + move(
        of(1, 1).astype(BF), dx=1, dc=1
    ).astype(F32)
    return jnp.where(
        c == 0,
        jnp.concatenate([same, cross], axis=1),
        jnp.concatenate([cross, same], axis=1),
    )


def per_device(queries, keys, values, positions, out_weight, cotangent):
    blk = lax.axis_index("blk")
    tp = lax.axis_index("tp")
    c = blk % NC
    a = blk // NC % NX
    z = blk // (NC * NX) % NZ
    y = blk // (NC * NX * NZ)
    width = queries.shape[1]
    half = width // 2
    shard = out_weight.shape[0]
    positions = positions[:, None]
    first = (c * (half // HD)).astype(jnp.int32)[None]

    def at_y(d):
        to = (y + d) % NY
        return (to // 2 + tp) % 2 * 2 + to % 2

    def at_z(d):
        return (z + d) % NZ

    def swap(x):
        return lax.ppermute(x, "tp", [(0, 1), (1, 0)])

    done = {}

    def forward(up, down):
        pos = tie(positions, up, down)
        done["att"], done["p"] = attend(first, queries, keys, values, pos)
        return (done["att"],)

    def grad_of_sibling(up, down):
        att_o = done["att"][:, half:]
        own_o = dot(tie(cotangent, up, down), att_o, TN).astype(BF)
        other_o = dot(tie(cot_other, up, down), att_o, TN).astype(BF)
        done["sent"] = jnp.concatenate([own_o, other_o], axis=0)
        return (done["sent"],)

    def grad_of_core(up, down):
        att_c = done["att"][:, :half]
        done["got"] = move(tie(done["sent"], up, down), dc=1)
        own_c = dot(tie(cotangent, up, down), att_c, TN).astype(BF)
        other_c = dot(tie(cot_other, up, down), att_c, TN).astype(BF)
        g = jnp.concatenate([own_c, other_c], axis=0).astype(F32)
        g = (g + done["got"].astype(F32)).astype(BF)
        done["ring"] = reduce_ring(
            g.reshape(NY, NZ, NX * NC * shard, half), 0, y_step, NY, at_y, rows(NZ // 2)
        )
        done["sends"] = next(done["ring"])
        return done["sends"]

    block = gather_chips(out_weight, a, c)
    cot_other = swap(tie(cotangent, block))
    block = gather_direct(block, y_step, NY, at_y, 0)
    blocks, places = gather_ring(
        block, z_step, NZ, at_z, [forward, grad_of_sibling, grad_of_core]
    )
    att, ring = done["att"], done["ring"]

    def back(part, grad_attended, into=()):
        return attend_back(
            first, part, done["p"], queries, keys, values, att, grad_attended, into
        )

    sends = ring.send(())
    blocks[-1] = tie(blocks[-1], *sends)
    weight_c = assemble(blocks, places, NZ).reshape(2 * width, half)
    weight_o = move(weight_c, dc=1)
    ga_c = grad_attended_half(cotangent, tie(cot_other, *sends), weight_c)
    partial = project(att, weight_c, tie(weight_o, ga_c), 1)
    got = swap(partial)
    grads = back(0, tie(ga_c, partial, *sends))
    g = ring.send(tuple(grads)).astype(BF)

    ring = reduce_ring(g, 0, z_step, NZ, at_z, columns(CUT))
    sends = next(ring)
    ga_o = grad_attended_half(cotangent, tie(cot_other, *sends), weight_o)
    sends = ring.send((ga_o,))
    grads = back(1, tie(ga_o, *sends), grads)
    sends = ring.send(tuple(grads))
    projected = project(att, weight_c, weight_o, 0, tie(got, *sends))
    sends = ring.send((projected,))
    r = ring.send(())
    weight_grad = reduce_chips(r.reshape(NX, NC, shard, half), a, c)
    return (projected, weight_grad, *grads)


def solution(mesh):
    spec = P("blk", "tp")
    return jax.shard_map(
        per_device,
        mesh=mesh,
        in_specs=(spec, spec, spec, P("blk"), spec, spec),
        out_specs=(spec,) * 5,
        check_vma=False,
    )
```

```python
import functools
import math

import jax
import jax.numpy as jnp
from jax import lax
from jax.experimental import pallas as pl
from jax.experimental.pallas import tpu as pltpu
from jax.sharding import PartitionSpec as P

HD = 128
NY, NZ, NX, NC = 4, 8, 2, 2
BF = jnp.bfloat16
F32 = jnp.float32
NT = (((1,), (1,)), ((), ()))
TN = (((0,), (0,)), ((), ()))
CUT = 384
QB = 256


def dot(a, b, dims=(((1,), (0,)), ((), ()))):
    return lax.dot_general(a, b, dims, preferred_element_type=F32)


def attend_kernel(first_ref, pos_ref, q_ref, k_ref, v_ref, att_ref, p_ref):
    length = q_ref.shape[0]
    for i in range(length // QB):
        rows = slice(i * QB, (i + 1) * QB)
        n = (i + 1) * QB
        s = dot(q_ref[rows, :], k_ref[:n, :], NT)
        row = lax.broadcasted_iota(jnp.int32, (QB, n), 0) + i * QB
        col = lax.broadcasted_iota(jnp.int32, (QB, n), 1)
        first = row - pos_ref[rows, :]
        s = jnp.where((col <= row) & (col >= first), s, -jnp.inf)
        e = jnp.exp((s - jnp.max(s, axis=-1, keepdims=True)) * (1.0 / math.sqrt(HD)))
        p = (e * (1.0 / jnp.sum(e, axis=-1, keepdims=True))).astype(BF)
        p_ref[0, rows, :n] = p
        att_ref[rows, :] = dot(p, v_ref[:n, :]).astype(BF)


def head_specs(length, heads):
    plain = pl.BlockSpec((length, HD), lambda h, first: (0, (first[0] + h) % heads))
    turned = pl.BlockSpec((length, HD), lambda h, first: (0, h))
    square = pl.BlockSpec((1, length, length), lambda h, first: (h, 0, 0))
    return plain, turned, square


def attend(first, queries, keys, values, positions):
    length, width = queries.shape
    heads = width // HD
    plain, turned, square = head_specs(length, heads)
    return pl.pallas_call(
        attend_kernel,
        grid_spec=pltpu.PrefetchScalarGridSpec(
            num_scalar_prefetch=1,
            grid=(heads,),
            in_specs=[pl.BlockSpec((length, 1), lambda h, first: (0, 0))] + [plain] * 3,
            out_specs=[turned, square],
        ),
        out_shape=[
            jax.ShapeDtypeStruct((length, width), BF),
            jax.ShapeDtypeStruct((heads, length, length), BF),
        ],
        compiler_params=pltpu.CompilerParams(vmem_limit_bytes=32 << 20),
        name="attend",
    )(first, positions, queries, keys, values)


def attend_back_kernel(first_ref, p_ref, q_ref, k_ref, v_ref, att_ref, ga_ref, *refs):
    dq_ref, dk_ref, dv_ref = refs[-3:]
    length = q_ref.shape[0]
    dk = dv = None
    for i in reversed(range(length // QB)):
        rows = slice(i * QB, (i + 1) * QB)
        n = (i + 1) * QB
        p = p_ref[0, rows, :n]
        ga = ga_ref[rows, :]
        delta = jnp.sum(
            ga.astype(F32) * att_ref[rows, :].astype(F32), axis=-1, keepdims=True
        )
        gp = dot(ga, v_ref[:n, :], NT)
        ds = ((1.0 / math.sqrt(HD)) * p.astype(F32) * (gp - delta)).astype(BF)
        dq_ref[rows, :] = dot(ds, k_ref[:n, :]).astype(BF)
        dk_i = dot(ds, q_ref[rows, :], TN)
        dv_i = dot(p, ga, TN)
        if dk is None:
            dk, dv = dk_i, dv_i
        else:
            dk_ref[n:, :] = dk[n:].astype(BF)
            dv_ref[n:, :] = dv[n:].astype(BF)
            dk, dv = dk[:n] + dk_i, dv[:n] + dv_i
    n = dk.shape[0]
    dk_ref[:n, :] = dk.astype(BF)
    dv_ref[:n, :] = dv.astype(BF)


def attend_back(first, part, probabilities, queries, keys, values, attended, grad_attended, into=()):
    length, width = queries.shape
    heads = width // HD
    n = heads // 2
    plain = pl.BlockSpec((length, HD), lambda h, first: (0, (first[0] + part * n + h) % heads))
    turned = pl.BlockSpec((length, HD), lambda h, first: (0, part * n + h))
    of_part = pl.BlockSpec((length, HD), lambda h, first: (0, h))
    square = pl.BlockSpec((1, length, length), lambda h, first: (part * n + h, 0, 0))
    out = jax.ShapeDtypeStruct((length, width), BF)
    return pl.pallas_call(
        attend_back_kernel,
        grid_spec=pltpu.PrefetchScalarGridSpec(
            num_scalar_prefetch=1,
            grid=(n,),
            in_specs=[square] + [plain] * 3 + [turned, of_part]
            + [pl.BlockSpec(memory_space=pl.ANY)] * len(into),
            out_specs=[plain] * 3,
        ),
        out_shape=[out] * 3,
        input_output_aliases={7 + k: k for k in range(len(into))},
        compiler_params=pltpu.CompilerParams(vmem_limit_bytes=56 << 20),
        name="attend_back",
    )(first, probabilities, queries, keys, values, attended, grad_attended, *into)


FB = 256


def grad_attended_half(cot_own, cot_other, weight):
    length, width = cot_own.shape
    half = weight.shape[1]
    n = width // half

    def kernel(own_ref, other_ref, w_ref, out_ref, acc_ref):
        i = pl.program_id(0)

        @pl.when(i == 0)
        def _():
            acc_ref[...] = dot(own_ref[...], w_ref[...])

        @pl.when((i > 0) & (i < n))
        def _():
            acc_ref[...] += dot(own_ref[...], w_ref[...])

        @pl.when((i >= n) & (i < 2 * n - 1))
        def _():
            acc_ref[...] += dot(other_ref[...], w_ref[...])

        @pl.when(i == 2 * n - 1)
        def _():
            out_ref[...] = (acc_ref[...] + dot(other_ref[...], w_ref[...])).astype(BF)

    return pl.pallas_call(
        kernel,
        grid=(2 * n,),
        in_specs=[
            pl.BlockSpec((length, half), lambda i: (0, jnp.minimum(i, n - 1))),
            pl.BlockSpec((length, half), lambda i: (0, jnp.maximum(i - n, 0))),
            pl.BlockSpec((half, half), lambda i: (i, 0)),
        ],
        out_specs=pl.BlockSpec((length, half), lambda i: (0, 0)),
        out_shape=jax.ShapeDtypeStruct((length, half), BF),
        scratch_shapes=[pltpu.VMEM((length, half), F32)],
        compiler_params=pltpu.CompilerParams(vmem_limit_bytes=32 << 20),
        name="grad_attended_half",
    )(cot_own, cot_other, weight)


def project(att, weight_c, weight_o, side, got=None):
    length, width = att.shape
    half = width // 2
    n = width // FB

    def kernel(att_ref, wc_ref, wo_ref, *refs):
        p = dot(att_ref[:, :half], wc_ref[...], NT) + dot(att_ref[:, half:], wo_ref[...], NT)
        if got is not None:
            p = p + refs[0][...].astype(F32)
        refs[-1][...] = p.astype(BF)

    block = pl.BlockSpec((length, FB), lambda i: (0, i))
    rows_of = pl.BlockSpec((FB, half), lambda i: (side * n + i, 0))
    more = [] if got is None else [got]
    return pl.pallas_call(
        kernel,
        grid=(n,),
        in_specs=[pl.BlockSpec((length, width), lambda i: (0, 0)), rows_of, rows_of]
        + [block] * len(more),
        out_specs=block,
        out_shape=jax.ShapeDtypeStruct((length, width), BF),
        compiler_params=pltpu.CompilerParams(vmem_limit_bytes=32 << 20),
        name="project",
    )(att, weight_c, weight_o, *more)


def move(x, dy=0, dz=0, dx=0, dc=0):
    pairs = []
    for y in range(NY):
        for z in range(NZ):
            for a in range(NX):
                for c in range(NC):
                    src = ((y * NZ + z) * NX + a) * NC + c
                    dst = (
                        ((y + dy) % NY * NZ + (z + dz) % NZ) * NX + (a + dx) % NX
                    ) * NC + (c + dc) % NC
                    pairs.append((src, dst))
    return lax.ppermute(x, "blk", pairs)


def pick(x, index, axis):
    return lax.dynamic_index_in_dim(x, index, axis, keepdims=False)


def put(buffer, block, index, axis):
    return lax.dynamic_update_index_in_dim(buffer, block, index, axis)


def y_step(x, d):
    return move(x, dy=d)


def z_step(x, d):
    return move(x, dz=d)


def tie(x, *others):
    return lax.optimization_barrier((x,) + others)[0]


def assemble(blocks, places, n):
    *whole, first, last = blocks
    k = whole[0].shape[0]

    def kernel(place_ref, *refs):
        *block_refs, first_ref, last_ref, out_ref = refs
        for i, ref in enumerate(block_refs):
            out_ref[:, place_ref[i]] = ref[...]
        at = place_ref[n - 1]
        out_ref[: k // 2, at] = first_ref[...]
        out_ref[k // 2 :, at] = last_ref[...]

    vmem = pl.BlockSpec(memory_space=pltpu.VMEM)
    return pl.pallas_call(
        kernel,
        in_specs=[pl.BlockSpec(memory_space=pltpu.SMEM)] + [vmem] * len(blocks),
        out_specs=vmem,
        out_shape=jax.ShapeDtypeStruct((k, n) + whole[0].shape[1:], whole[0].dtype),
        compiler_params=pltpu.CompilerParams(vmem_limit_bytes=32 << 20),
        name="assemble",
    )(jnp.stack(places).astype(jnp.int32), *blocks)


def gather_ring(x, step, n, at, beside):
    blocks, places = [x], [at(0)]
    up = down = x
    for d in range(1, n // 2):
        work = beside[d - 1](up, down)
        up, down = step(up, 1), step(down, -1)
        blocks += [up, down]
        places += [at(-d), at(d)]
        up, down = lax.optimization_barrier((up, down) + tuple(work))[:2]
    k = x.shape[0] // 2
    return blocks + [step(up[:k], 1), step(down[k:], -1)], places + [at(n // 2)]


def gather_direct(x, step, n, at, axis):
    shape = x.shape[:axis] + (n,) + x.shape[axis:]
    out = jnp.broadcast_to(jnp.expand_dims(x, axis), shape)
    for d in range(1, n):
        out = put(out, step(x, d), at(-d), axis)
    return out


def reduce_ring(x, axis, step, n, at, cut):
    split, join = cut

    def block(d):
        return pick(x, at(d), axis)

    def add(u, w):
        return (u.astype(F32) + w.astype(F32)).astype(x.dtype)

    up, down = split(block(n // 2))
    for d in range(n // 2 - 1, -1, -1):
        beside = yield up, down
        up, down = step(up, 1), step(down, -1)
        if beside:
            up, down = lax.optimization_barrier((up, down) + tuple(beside))[:2]
        if d == 0:
            yield block(0).astype(F32) + up.astype(F32) + down.astype(F32)
        elif d == n // 2 - 1:
            u, w = split(block(d))
            v, t = split(block(-d))
            up, down = join(add(u, up), w), join(v, add(t, down))
        else:
            up, down = add(block(d), up), add(block(-d), down)


def columns(at):
    return (
        lambda x: (x[..., :at], x[..., at:]),
        lambda u, w: jnp.concatenate([u, w], axis=-1),
    )


def rows(at):
    return lambda x: (x[:at], x[at:]), lambda u, w: jnp.concatenate([u, w], axis=0)


def gather_chips(weight, a, c):
    shard, width = weight.shape
    half = width // 2
    mine = lax.dynamic_slice_in_dim(weight, c * half, half, 1)
    other = lax.dynamic_slice_in_dim(weight, (1 - c) * half, half, 1)
    from_a = move(mine, dx=1)
    from_c = move(other, dc=1)
    from_ac = move(other, dx=1, dc=1)
    here = jnp.where(c == 0, jnp.stack([mine, from_c]), jnp.stack([from_c, mine]))
    there = jnp.where(c == 0, jnp.stack([from_a, from_ac]), jnp.stack([from_ac, from_a]))
    block = jnp.where(a == 0, jnp.concatenate([here, there]), jnp.concatenate([there, here]))
    return block.reshape(NX * NC * shard, half)


def reduce_chips(r, a, c):
    def of(da, dc):
        return pick(pick(r, (a + da) % NX, 0), (c + dc) % NC, 0)

    same = of(0, 0) + move(of(1, 0).astype(BF), dx=1).astype(F32)
    cross = move(of(0, 1).astype(BF), dc=1).astype(F32) + move(
        of(1, 1).astype(BF), dx=1, dc=1
    ).astype(F32)
    return jnp.where(
        c == 0,
        jnp.concatenate([same, cross], axis=1),
        jnp.concatenate([cross, same], axis=1),
    )


def per_device(queries, keys, values, positions, out_weight, cotangent):
    blk = lax.axis_index("blk")
    tp = lax.axis_index("tp")
    c = blk % NC
    a = blk // NC % NX
    z = blk // (NC * NX) % NZ
    y = blk // (NC * NX * NZ)
    width = queries.shape[1]
    half = width // 2
    shard = out_weight.shape[0]
    positions = positions[:, None]
    first = (c * (half // HD)).astype(jnp.int32)[None]

    def at_y(d):
        to = (y + d) % NY
        return (to // 2 + tp) % 2 * 2 + to % 2

    def at_z(d):
        return (z + d) % NZ

    def swap(x):
        return lax.ppermute(x, "tp", [(0, 1), (1, 0)])

    done = {}

    def forward(up, down):
        pos = tie(positions, up, down)
        done["att"], done["p"] = attend(first, queries, keys, values, pos)
        return (done["att"],)

    def grad_of_sibling(up, down):
        att_o = done["att"][:, half:]
        own_o = dot(tie(cotangent, up, down), att_o, TN).astype(BF)
        other_o = dot(tie(cot_other, up, down), att_o, TN).astype(BF)
        done["sent"] = jnp.concatenate([own_o, other_o], axis=0)
        return (done["sent"],)

    def grad_of_core(up, down):
        att_c = done["att"][:, :half]
        done["got"] = move(tie(done["sent"], up, down), dc=1)
        own_c = dot(tie(cotangent, up, down), att_c, TN).astype(BF)
        other_c = dot(tie(cot_other, up, down), att_c, TN).astype(BF)
        g = jnp.concatenate([own_c, other_c], axis=0).astype(F32)
        g = (g + done["got"].astype(F32)).astype(BF)
        done["ring"] = reduce_ring(
            g.reshape(NY, NZ, NX * NC * shard, half), 0, y_step, NY, at_y, rows(NZ // 2)
        )
        done["sends"] = next(done["ring"])
        return done["sends"]

    block = gather_chips(out_weight, a, c)
    cot_other = swap(tie(cotangent, block))
    block = gather_direct(block, y_step, NY, at_y, 0)
    blocks, places = gather_ring(
        block, z_step, NZ, at_z, [forward, grad_of_sibling, grad_of_core]
    )
    att, ring = done["att"], done["ring"]

    def back(part, grad_attended, into=()):
        return attend_back(
            first, part, done["p"], queries, keys, values, att, grad_attended, into
        )

    sends = ring.send(())
    blocks[-1] = tie(blocks[-1], *sends)
    weight_c = assemble(blocks, places, NZ).reshape(2 * width, half)
    weight_o = move(weight_c, dc=1)
    ga_c = grad_attended_half(cotangent, tie(cot_other, *sends), weight_c)
    partial = project(att, weight_c, tie(weight_o, ga_c), 1)
    got = swap(partial)
    grads = back(0, tie(ga_c, partial, *sends))
    g = ring.send(tuple(grads)).astype(BF)

    ring = reduce_ring(g, 0, z_step, NZ, at_z, columns(CUT))
    sends = next(ring)
    ga_o = grad_attended_half(cotangent, tie(cot_other, *sends), weight_o)
    sends = ring.send((ga_o,))
    grads = back(1, tie(ga_o, *sends), grads)
    sends = ring.send(tuple(grads))
    projected = project(att, weight_c, weight_o, 0, tie(got, *sends))
    sends = ring.send((projected,))
    r = ring.send(())
    weight_grad = reduce_chips(r.reshape(NX, NC, shard, half), a, c)
    return (projected, weight_grad, *grads)


def solution(mesh):
    spec = P("blk", "tp")
    return jax.shard_map(
        per_device,
        mesh=mesh,
        in_specs=(spec, spec, spec, P("blk"), spec, spec),
        out_specs=(spec,) * 5,
        check_vma=False,
    )
```
